32 devices in a mesh: expert: 4 (over y, x), dp: 8 (over z, core).
Axes of the slice: x: 2, y: 2, z: 4, core: 2. Of those that a mesh axis runs over, the one named last changes fastest.
Arguments:
- inputs: bfloat16 [32768, 768], P(('expert', 'dp')), may hold values from -6 to 6
- gain_attn: bfloat16 [768], P('dp'), may hold values from 0.5 to 1.5
- w_query: bfloat16 [768, 768], P('dp'), may hold values from -0.109375 to 0.109375
- w_key: bfloat16 [768, 768], P('dp'), may hold values from -0.109375 to 0.109375
- w_value: bfloat16 [768, 768], P('dp'), may hold values from -0.21875 to 0.21875
- w_output: bfloat16 [768, 768], P('dp'), may hold values from -0.875 to 0.875
- bias_table: bfloat16 [32, 12], P('dp'), may hold values from -6 to 6
- gain_ffn: bfloat16 [768], P('dp'), may hold values from 0.5 to 1.5
- w_router: bfloat16 [768, 32], P('dp'), may hold values from -0.109375 to 0.109375
- w_in: bfloat16 [32, 3072, 768], P('expert'), may hold values from -0.21875 to 0.21875
- w_out: bfloat16 [32, 3072, 768], P('expert'), may hold values from -4 to 4
- segments: int32 [32, 1024], P(('expert', 'dp')), may hold values from 0 to 3, never falling along the last dimension, each value on 1 to 512 neighbouring positions
- buckets: int32 [1024, 1024], replicated, may hold values from 0 to 31, as said below
- routes: int32 [32768], P(('expert', 'dp')), may hold values from 0 to 31, as said below
- slot_ids: int32 [32768], P(('expert', 'dp')), may hold values from 0 to 63, as said below
- cotangent: bfloat16 [32768, 768], P(('expert', 'dp')), may hold values from -6 to 6
Outputs:
- output: bfloat16 [32768, 768], P(('expert', 'dp'))
- grad_inputs: bfloat16 [32768, 768], P(('expert', 'dp'))
- grad_gain_attn: float32 [768], P('dp')
- grad_w_query: float32 [768, 768], P('dp')
- grad_w_key: float32 [768, 768], P('dp')
- grad_w_value: float32 [768, 768], P('dp')
- grad_w_output: float32 [768, 768], P('dp')
- grad_bias_table: float32 [32, 12], P('dp')
- grad_gain_ffn: float32 [768], P('dp')
- grad_w_router: float32 [768, 32], P('dp')
- grad_w_in: float32 [32, 3072, 768], P('expert', 'dp')
- grad_w_out: float32 [32, 3072, 768], P('expert', 'dp')
The draws below stay inside these ranges and needn't reach their ends.
Inputs may be any that keep to these rules, and one draw needn't show every extreme that they name: `routes`: within the 1024 tokens of one device no expert is named more than 64 times, and on every device one expert is named exactly 64 times. `slot_ids`: two tokens of one device with the same expert never share a slot. `buckets`: depends only on j - i; 0 where j = i, below 16 where j < i and 16 or more where j > i; never falls as the distance grows on either side. `segments`: never falls along a sequence.
All inputs are finite; a program needn't handle non-finite values.
Results may differ from the reference program's by a relative error of at most 0.02.
Values may be sent and summed in bfloat16 or wider, within the bound.
A program may use at most 512 MiB of HBM per device.

```python
import math
import jax
import jax.numpy as jnp
import numpy as np
from jax import lax

D = 768
H = 12
DH = 64
FF = 3072
E = 32
NB = 32
SEQ_LEN = 1024
TOK_DEV = 1024
CAP = 64
SEQS = 32
TOKENS = 32768
N_EXPERT = 4
N_DP = 8


def route_table(key):
    block_count = N_EXPERT * N_DP
    slot_total = E * CAP
    hot_expert = jax.random.randint(jax.random.fold_in(key, 1), (N_DP,), 0, E)
    hot_block = jnp.tile(hot_expert, N_EXPERT)
    slot_ranks = jax.vmap(lambda item: jax.random.permutation(item, slot_total))(jax.random.split(jax.random.fold_in(key, 2), block_count))
    slot_owner = jnp.arange(slot_total, dtype=jnp.int32) // CAP
    slot_score = slot_ranks.astype(jnp.int32) + slot_total * (slot_owner[None, :] != hot_block[:, None]).astype(jnp.int32)
    slot_order = jnp.argsort(slot_score, axis=1, stable=True)[:, :TOK_DEV]
    mixing = jax.vmap(lambda item: jax.random.permutation(item, TOK_DEV))(jax.random.split(jax.random.fold_in(key, 3), block_count))
    chosen = jnp.take_along_axis(slot_order, mixing.astype(jnp.int32), axis=1)
    chosen = chosen.reshape(-1).astype(jnp.int32)
    return (chosen // CAP, chosen % CAP)


def draw_routes(key, part):
    shared = route_table(key)
    return shared[0]


def draw_slot_ids(key, part):
    shared = route_table(key)
    return shared[1]


def draw_buckets(key, part):
    key = jax.random.fold_in(key, 11)
    jitter = jax.random.randint(key, (7,), -1, 2)
    bounds = jnp.array([10, 13, 17, 22, 29, 38, 50], dtype=jnp.int32) + jitter.astype(jnp.int32)
    places = jnp.arange(SEQ_LEN, dtype=jnp.int32)
    offset = places[None, :] - places[:, None]
    distance = jnp.abs(offset)
    far_bucket = 8 + jnp.sum((distance[:, :, None] >= bounds[None, None, :]).astype(jnp.int32), axis=-1)
    near_bucket = jnp.where(distance < 8, distance, far_bucket)
    return (near_bucket + 16 * (offset > 0).astype(jnp.int32)).astype(jnp.int32)


def shard_levels(key, dims, cuts, smallest, high):
    def one(position, blocks):
        steps = jax.random.uniform(jax.random.fold_in(jax.random.fold_in(key, 6), position), (blocks,), jnp.float32, smallest / len(cuts), high / len(cuts))
        return jnp.repeat(jnp.exp(steps), dims[position] // blocks).reshape((-1,) + (1,) * (len(dims) - position - 1))

    loudness = one(*cuts[0])
    for cut in cuts[1:]:
        loudness = loudness * one(*cut)
    return loudness


def split_up(amount, total, most, lean):
    loads = [(1 << 20) // math.isqrt(grade ** lean) + 1 for grade in range(2, amount + 1)]
    surplus, counts = total - most - (amount - 1), [1] * (amount - 1)
    while surplus > 0:
        candidates = [i for i in range(amount - 1) if counts[i] < most]
        whole, left = sum([loads[i] for i in candidates]), surplus
        for i in candidates:
            more = min(most - counts[i], max(1, left * loads[i] // whole), surplus)
            counts[i] = counts[i] + more
            surplus = surplus - more
    return np.array([most] + counts)


def uneven_parts(key, count, total, limit, skew):
    if count == 2:
        one = jax.random.randint(key, (), max(1, total - limit), min(limit, total - 1) + 1)
        return jnp.stack([one, total - one])
    tallies = jnp.asarray(split_up(count, total, limit, skew), jnp.int32)
    couples = (count - 1) // 2
    donor, sink = tallies[1:1 + 2 * couples:2], tallies[2:2 + 2 * couples:2]
    room = jnp.minimum(donor - 1, limit - sink)
    passed = jax.random.randint(jax.random.fold_in(key, 1), (couples,), 0, 1 << 20) % (room + 1)
    tallies = tallies.at[1:1 + 2 * couples:2].set(donor - passed).at[2:2 + 2 * couples:2].set(sink + passed)
    return tallies[jax.random.permutation(jax.random.fold_in(key, 2), count)]


def bell_draw(own_key, extent, deviation, bound, cuts=(), kind=jnp.bfloat16):
    loudness = shard_levels(own_key, extent, cuts, -0.22, 0.18) if cuts else 1.0
    drawn = jax.random.normal(own_key, extent, jnp.float32) * deviation * loudness
    return jnp.minimum(jnp.maximum(drawn, -bound), bound).astype(kind)


def setup_inputs(seed: int = 0) -> dict:
    key_list = jax.random.split(jax.random.key(seed), 17)
    return {
        "inputs": bell_draw(key_list[0], (TOKENS, D), 1.0, 6.0, ((0, 32),)),
        "gain_attn": jnp.clip(1.0 + 0.1 * jax.random.normal(key_list[1], (D,), jnp.float32), 0.5, 1.5).astype(jnp.bfloat16),
        "w_query": bell_draw(key_list[2], (D, H * DH), (4 * D) ** -0.5, 0.109375, ((0, 8),)),
        "w_key": bell_draw(key_list[3], (D, H * DH), (4 * D) ** -0.5, 0.109375, ((0, 8),)),
        "w_value": bell_draw(key_list[4], (D, H * DH), D ** -0.5, 0.21875, ((0, 8),)),
        "w_output": bell_draw(key_list[5], (H * DH, D), (D // 16) ** -0.5, 0.875, ((0, 8),)),
        "bias_table": bell_draw(key_list[6], (NB, H), 1.0, 6.0, ((0, 8),)),
        "gain_ffn": jnp.clip(1.0 + 0.1 * jax.random.normal(key_list[7], (D,), jnp.float32), 0.5, 1.5).astype(jnp.bfloat16),
        "w_router": bell_draw(key_list[8], (D, E), (4 * D) ** -0.5, 0.109375, ((0, 8),)),
        "w_in": bell_draw(key_list[9], (E, FF, D), D ** -0.5, 0.21875, ((0, 4),)),
        "w_out": bell_draw(key_list[10], (E, FF, D), (max(FF // 1536, 1)) ** -0.5, 4.0, ((0, 4),)),
        "segments": jax.vmap(lambda own: jnp.searchsorted(jnp.cumsum(uneven_parts(own, max(SEQ_LEN // 256, 3), SEQ_LEN, SEQ_LEN // 2, 1)), jnp.arange(SEQ_LEN), side="right"))(jax.random.split(key_list[11], SEQS)).reshape((SEQS, SEQ_LEN)).astype(jnp.int32),
        "buckets": draw_buckets(jax.random.fold_in(key_list[16], 71), 0),
        "routes": draw_routes(jax.random.fold_in(key_list[16], 71), 0),
        "slot_ids": draw_slot_ids(jax.random.fold_in(key_list[16], 71), 0),
        "cotangent": bell_draw(key_list[15], (TOKENS, D), 1.0, 6.0, ((0, 32),)),
    }


@jax.custom_vjp
def low(v):
    return lax.optimization_barrier(v.astype(jnp.bfloat16)).astype(jnp.float32)

@jax.custom_vjp
def low_back(v):
    return v

def low_keep(v):
    return (low(v), None)

def low_pass(kept, grad):
    return (grad,)

def back_keep(v):
    return (v, None)

def back_low(kept, grad):
    return (low(grad),)
low.defvjp(low_keep, low_pass)
low_back.defvjp(back_keep, back_low)
epsilon = 1e-06
highest = lax.Precision.HIGHEST

def rounded_both(value):
    return low(low_back(value))

def rms_norm(value, gain):
    return value * lax.rsqrt(lax.optimization_barrier(jnp.mean(value * value, axis=-1, keepdims=True)) + epsilon) * gain

def attend_sequence(query, key_rows, value_rows, doc_ids, pos_bias):
    scores = jnp.einsum('qhd,khd->hqk', query, key_rows, precision=highest) + pos_bias
    scores = low_back(scores)
    same_doc = doc_ids[:, None] == doc_ids[None, :]
    scores = jnp.where(same_doc[None], scores, -1000000000.0)
    attn_probs = low(jax.nn.softmax(scores, axis=-1))
    return jnp.einsum('hqk,khd->qhd', attn_probs, value_rows, precision=highest)

def expert_block(rows_in, weight_in, weight_out):
    hidden = low_back(jnp.einsum('rd,fd->rf', rows_in, weight_in, precision=highest))
    activated = low(jax.nn.gelu(hidden, approximate=True))
    return rounded_both(jnp.einsum('rf,fd->rd', activated, weight_out, precision=highest))

def forward(inputs, gain_attn, w_query, w_key, w_value, w_output, bias_table, gain_ffn, w_router, w_in, w_out, segments, buckets, routes, slot_ids):
    token_count = inputs.shape[0]
    normed = low(rms_norm(inputs, gain_attn))
    query = rounded_both(jnp.dot(normed, w_query, precision=highest)).reshape(SEQS, SEQ_LEN, H, DH)
    key_rows = rounded_both(jnp.dot(normed, w_key, precision=highest)).reshape(SEQS, SEQ_LEN, H, DH)
    value_rows = rounded_both(jnp.dot(normed, w_value, precision=highest)).reshape(SEQS, SEQ_LEN, H, DH)
    pos_bias = jnp.transpose(bias_table[buckets], (2, 0, 1))
    checked = jax.checkpoint(attend_sequence)
    attended = lax.map(lambda item: checked(item[0], item[1], item[2], item[3], pos_bias), (query, key_rows, value_rows, segments))
    attended = rounded_both(attended.reshape(token_count, H * DH))
    branch = low_back(jnp.dot(attended, w_output, precision=highest))
    middle = inputs + branch
    normed2 = low(rms_norm(middle, gain_ffn))
    logits = low_back(jnp.dot(normed2, w_router, precision=highest))
    router_probs = jax.nn.softmax(logits, axis=-1)
    match = routes[:, None] == jnp.arange(E, dtype=jnp.int32)[None, :]
    gate_value = lax.optimization_barrier(jnp.sum(jnp.where(match, router_probs, 0.0), axis=-1))
    column = jnp.arange(token_count, dtype=jnp.int32) // TOK_DEV * CAP + slot_ids
    expert_rows = jnp.zeros((E, N_EXPERT * N_DP * CAP, D), inputs.dtype).at[routes, column].set(normed2)
    expert_rows = low_back(expert_rows)
    checked_expert = jax.checkpoint(expert_block)
    produced = lax.map(lambda item: checked_expert(item[0], item[1], item[2]), (expert_rows, w_in, w_out))
    returned = produced[routes, column]
    return middle + gate_value[:, None] * returned

def reference(inputs, gain_attn, w_query, w_key, w_value, w_output, bias_table, gain_ffn, w_router, w_in, w_out, segments, buckets, routes, slot_ids, cotangent):
    floats = tuple((item.astype(jnp.float32) for item in (inputs, gain_attn, w_query, w_key, w_value, w_output, bias_table, gain_ffn, w_router, w_in, w_out)))

    def closed(*weights):
        return forward(*weights, segments, buckets, routes, slot_ids)
    output, pull_back = jax.vjp(closed, *floats)
    gradients = pull_back(cotangent.astype(jnp.float32))
    return (output.astype(jnp.bfloat16), gradients[0].astype(jnp.bfloat16), gradients[1], gradients[2], gradients[3], gradients[4], gradients[5], gradients[6], gradients[7], gradients[8], gradients[9], gradients[10])
```

```python
import functools

import jax
import jax.numpy as jnp
from jax import lax
from jax.experimental import pallas as pl
from jax.experimental.pallas import tpu as pltpu
from jax.sharding import PartitionSpec as P

CAP = 64


epsilon = 1e-06


def diagonal_buckets(buckets):
    length = buckets.shape[0]
    return jnp.concatenate([buckets[length - 1, : length - 1], buckets[0], buckets[0, -1:]])


LANES = 128


def bias_strip(diagonal):
    wide = jnp.broadcast_to(diagonal, (LANES, diagonal.shape[1]))
    return pltpu.roll(wide, wide.shape[1] - (LANES - 1), 1, stride=1, stride_axis=0)


def head_scores(q, key, strip, first, docs_rows, docs_seq):
    length = key.shape[0]
    tiles = []
    for row in range(first, first + q.shape[0], LANES):
        start = length - LANES - row
        tiles.append(strip[:, start : start + length])
    raw = dot_nt(q, key) + jnp.concatenate(tiles, axis=0)
    return jnp.where(docs_rows == docs_seq, raw, -1000000000.0)


def attend_kernel(size, rows, q_ref, k_ref, v_ref, diag_ref, col_ref, row_ref, out_ref, lse_ref):
    length = q_ref.shape[0]
    docs_seq = row_ref[0]
    for head in range(q_ref.shape[1] // size):
        own = slice(head * size, (head + 1) * size)
        key, value = k_ref[:, own], v_ref[:, own]
        strip = bias_strip(diag_ref[0, head : head + 1, :])
        for first in range(0, length, rows):
            part = slice(first, first + rows)
            scores = head_scores(q_ref[part, own], key, strip, first, col_ref[0, part, :], docs_seq)
            top = jnp.max(scores, axis=-1, keepdims=True)
            weights = jnp.exp(scores - top)
            total = jnp.sum(weights, axis=-1, keepdims=True)
            probs = (weights * (1.0 / total)).astype(jnp.bfloat16)
            out_ref[part, own] = dot_nn(probs, value).astype(jnp.bfloat16)
            lse_ref[0, 0, part, head : head + 1] = top + jnp.log(total)


def attend_back_kernel(
    size,
    rows,
    q_ref,
    k_ref,
    v_ref,
    grad_ref,
    diag_ref,
    col_ref,
    row_ref,
    lse_ref,
    gq_ref,
    gk_ref,
    gv_ref,
    gd_ref,
    sum_k,
    sum_v,
    sum_s,
):
    length = q_ref.shape[0]
    docs_seq = row_ref[0]
    sum_k[...] = jnp.zeros_like(sum_k)
    sum_v[...] = jnp.zeros_like(sum_v)
    for head in range(q_ref.shape[1] // size):
        own = slice(head * size, (head + 1) * size)
        key, value = k_ref[:, own], v_ref[:, own]
        strip = bias_strip(diag_ref[0, head : head + 1, :])
        sum_s[...] = jnp.zeros_like(sum_s)
        for first in range(0, length, rows):
            part = slice(first, first + rows)
            q, grad = q_ref[part, own], grad_ref[part, own]
            scores = head_scores(q, key, strip, first, col_ref[0, part, :], docs_seq)
            probs = jnp.exp(scores - lse_ref[0, 0, part, head : head + 1])
            sum_v[own, :] += dot_nn(grad.T, probs.astype(jnp.bfloat16))
            grad_probs = dot_nt(grad, value)
            mean = jnp.sum(probs * grad_probs, axis=-1, keepdims=True)
            grad_scores = (probs * (grad_probs - mean)).astype(jnp.bfloat16)
            gq_ref[part, own] = dot_nn(grad_scores, key).astype(jnp.bfloat16)
            sum_k[own, :] += dot_nn(q.T, grad_scores)
            for row in range(0, rows, LANES):
                start = length - LANES - first - row
                sum_s[:, start : start + length] += grad_scores[row : row + LANES].astype(
                    jnp.float32
                )
        folded = sum_s[...]
        width = folded.shape[1]
        half = LANES // 2
        while half >= 1:
            folded = folded[:half] + pltpu.roll(folded[half:], width - half, 1)
            half = half // 2
        gd_ref[0, 0, head : head + 1, :] = pltpu.roll(folded, LANES - 1, 1)
    gk_ref[...] = sum_k[...].T.astype(jnp.bfloat16)
    gv_ref[...] = sum_v[...].T.astype(jnp.bfloat16)


def attention_specs(tokens, length, width, size, whole):
    pack = LANES // size
    packs = width // LANES
    column = lambda k: pl.BlockSpec((length, LANES), lambda s, h: (s, h + k * packs))
    return dict(
        grid=(tokens // length, packs),
        qkv=[column(0), column(1), column(2)],
        rows=column(0),
        diag=pl.BlockSpec((1, pack, whole), lambda s, h: (h, 0, 0)),
        col=pl.BlockSpec((1, length, 1), lambda s, h: (s, 0, 0)),
        row=pl.BlockSpec((1, 1, length), lambda s, h: (s, 0, 0)),
        lse=pl.BlockSpec((1, 1, length, pack), lambda s, h: (s, h, 0, 0)),
    )


def attend(qkv, diagonals, segments, size):
    tokens, width = qkv.shape[0], qkv.shape[1] // 3
    seqs, length = segments.shape
    pack, packs = LANES // size, width // LANES
    whole = diagonals.shape[1]
    specs = attention_specs(tokens, length, width, size, whole)
    pairs = tokens * length * width
    return pl.pallas_call(
        functools.partial(attend_kernel, size, 256),
        grid=specs["grid"],
        in_specs=specs["qkv"] + [specs["diag"], specs["col"], specs["row"]],
        out_specs=[specs["rows"], specs["lse"]],
        out_shape=[
            jax.ShapeDtypeStruct((tokens, width), jnp.bfloat16),
            jax.ShapeDtypeStruct((seqs, packs, length, pack), jnp.float32),
        ],
        compiler_params=pltpu.CompilerParams(vmem_limit_bytes=56 * 2**20),
        cost_estimate=pl.CostEstimate(
            flops=16 * pairs, bytes_accessed=10 * qkv.size, transcendentals=pairs // size
        ),
        name="attend",
    )(
        qkv,
        qkv,
        qkv,
        diagonals.reshape(packs, pack, whole),
        segments[:, :, None],
        segments[:, None, :],
    )


def attend_back(qkv, grad, diagonals, segments, lse, size):
    tokens, width = grad.shape
    seqs, length = segments.shape
    pack, packs = LANES // size, width // LANES
    whole = diagonals.shape[1]
    specs = attention_specs(tokens, length, width, size, whole)
    pairs = tokens * length * width
    rows_shape = jax.ShapeDtypeStruct((tokens, width), jnp.bfloat16)
    gq, gk, gv, gd = pl.pallas_call(
        functools.partial(attend_back_kernel, size, 256),
        grid=specs["grid"],
        in_specs=specs["qkv"]
        + [specs["rows"], specs["diag"], specs["col"], specs["row"], specs["lse"]],
        out_specs=[specs["rows"]] * 3
        + [pl.BlockSpec((1, 1, pack, whole), lambda s, h: (s, h, 0, 0))],
        out_shape=[rows_shape] * 3 + [jax.ShapeDtypeStruct((seqs, packs, pack, whole), jnp.float32)],
        scratch_shapes=[
            pltpu.VMEM((LANES, length), jnp.float32),
            pltpu.VMEM((LANES, length), jnp.float32),
            pltpu.VMEM((LANES, whole), jnp.float32),
        ],
        compiler_params=pltpu.CompilerParams(vmem_limit_bytes=56 * 2**20),
        cost_estimate=pl.CostEstimate(
            flops=40 * pairs, bytes_accessed=16 * qkv.size, transcendentals=pairs // size
        ),
        name="attend_back",
    )(
        qkv,
        qkv,
        qkv,
        grad,
        diagonals.reshape(packs, pack, whole),
        segments[:, :, None],
        segments[:, None, :],
        lse,
    )
    return gq, gk, gv, jnp.sum(gd, axis=0).reshape(packs * pack, whole)


def norm_back(grad_norm, value, inverse, gain):
    scaled = grad_norm * gain
    grad_value = inverse * scaled - value * inverse * inverse * inverse * jnp.mean(
        scaled * value, axis=-1, keepdims=True
    )
    return (grad_value, jnp.sum(grad_norm * value * inverse, axis=0))


def to_column(parts, rows):
    return jnp.pad(parts, ((0, 0), (0, rows - parts.shape[1]))).reshape(-1, 1)


def from_column(column, count, shape):
    return column.reshape(count, -1)[:, : shape[0] * shape[1]].reshape(count * shape[0], shape[1])


def exchange(blocks, count, sign):
    got = [blocks[0]]
    for step in range(1, count):
        pairs = [(item, (item + sign * step) % count) for item in range(count)]
        got.append(lax.ppermute(blocks[step], "expert", pairs))
    return jnp.stack(got)


def gelu_both(v):
    square = v * v
    t = jnp.tanh(0.7978845608028654 * (v + 0.044715 * v * square))
    half = 0.5 * (1.0 + t)
    slope = half + 0.5 * v * (1.0 - t * t) * (0.7978845608028654 * (1.0 + 0.134145 * square))
    return v * half, slope


def dot_nt(a, b):
    return lax.dot_general(a, b, (((1,), (1,)), ((), ())), preferred_element_type=jnp.float32)


def dot_nn(a, b):
    return jnp.dot(a, b, preferred_element_type=jnp.float32)


def expert_kernel(x_ref, g_ref, in_ref, out_ref, p_ref, a_ref, sum_p, sum_a):
    part = pl.program_id(1)
    width = x_ref.shape[-1]
    x = x_ref[...].reshape(-1, width)
    g = g_ref[...].reshape(-1, width)
    value, slope = gelu_both(dot_nt(x, in_ref[0]))
    grad_hidden = (dot_nt(g, out_ref[0]) * slope).astype(jnp.bfloat16)
    made = dot_nn(value.astype(jnp.bfloat16), out_ref[0])
    back = dot_nn(grad_hidden, in_ref[0])

    @pl.when(part == 0)
    def _():
        sum_p[...] = made
        sum_a[...] = back

    @pl.when(part > 0)
    def _():
        sum_p[...] += made
        sum_a[...] += back

    @pl.when(part == pl.num_programs(1) - 1)
    def _():
        p_ref[...] = sum_p[...].astype(jnp.bfloat16).reshape(p_ref.shape)
        a_ref[...] = sum_a[...].astype(jnp.bfloat16).reshape(a_ref.shape)


def expert_rows(arrived, grad_produced, w_in, w_out):
    count, experts, cap, width = arrived.shape
    hidden = w_in.shape[1]
    part = hidden // 3 if hidden % 3 == 0 else hidden
    rows_spec = pl.BlockSpec((count, 1, cap, width), lambda e, f: (0, e, 0, 0))
    weight_spec = pl.BlockSpec((1, part, width), lambda e, f: (e, f, 0))
    return pl.pallas_call(
        expert_kernel,
        grid=(experts, hidden // part),
        in_specs=[rows_spec, rows_spec, weight_spec, weight_spec],
        out_specs=[rows_spec, rows_spec],
        out_shape=[jax.ShapeDtypeStruct(arrived.shape, jnp.bfloat16)] * 2,
        scratch_shapes=[pltpu.VMEM((count * cap, width), jnp.float32)] * 2,
        compiler_params=pltpu.CompilerParams(vmem_limit_bytes=56 * 2**20),
        cost_estimate=pl.CostEstimate(
            flops=8 * count * experts * cap * width * hidden,
            bytes_accessed=4 * experts * hidden * width + 8 * arrived.size,
            transcendentals=count * experts * cap * hidden,
        ),
        name="expert_rows",
    )(arrived, grad_produced, w_in, w_out)


def weight_kernel(x_ref, g_ref, in_ref, out_ref, gi_ref, go_ref):
    step = pl.program_id(1)
    width = x_ref.shape[-1]
    x = x_ref[...].reshape(-1, width)
    g = g_ref[...].reshape(-1, width)
    value, slope = gelu_both(dot_nt(in_ref[0], x))
    grad_hidden = (dot_nt(out_ref[0], g) * slope).astype(jnp.bfloat16)
    for_in = dot_nn(grad_hidden, x)
    for_out = dot_nn(value.astype(jnp.bfloat16), g)

    @pl.when(step == 0)
    def _():
        gi_ref[0] = for_in
        go_ref[0] = for_out

    @pl.when(step > 0)
    def _():
        gi_ref[0] += for_in
        go_ref[0] += for_out


def expert_weight_grads(arrived_all, grad_all, w_in, w_out):
    dp_count, count, experts, cap, width = arrived_all.shape
    hidden = w_in.shape[1]
    many = max(1, min(dp_count, 1024 // (count * cap)))
    rows_spec = pl.BlockSpec((many, count, 1, cap, width), lambda e, r: (r, 0, e, 0, 0))
    weight_spec = pl.BlockSpec((1, hidden, width), lambda e, r: (e, 0, 0))
    return pl.pallas_call(
        weight_kernel,
        grid=(experts, dp_count // many),
        in_specs=[rows_spec, rows_spec, weight_spec, weight_spec],
        out_specs=[weight_spec, weight_spec],
        out_shape=[jax.ShapeDtypeStruct((experts, hidden, width), jnp.float32)] * 2,
        compiler_params=pltpu.CompilerParams(vmem_limit_bytes=56 * 2**20),
        cost_estimate=pl.CostEstimate(
            flops=8 * arrived_all.size * hidden,
            bytes_accessed=4 * arrived_all.size + 12 * w_in.size,
            transcendentals=arrived_all.size // width * hidden,
        ),
        name="expert_weight_grads",
    )(arrived_all, grad_all, w_in, w_out)


def on_device(
    inputs,
    gain_attn,
    w_query,
    w_key,
    w_value,
    w_output,
    bias_table,
    gain_ffn,
    w_router,
    w_in,
    w_out,
    segments,
    buckets,
    routes,
    slot_ids,
    cotangent,
):
    dp_count = lax.axis_size("dp")
    group_count = lax.axis_size("expert")
    group = lax.axis_index("expert")
    shard = lax.axis_index("dp")
    shard_rows, head_count = w_query.shape[0], bias_table.shape[1]
    expert_count = w_router.shape[1]
    bucket_count = bias_table.shape[0] * dp_count
    small = jnp.concatenate(
        [
            gain_attn[:, None],
            gain_ffn[:, None],
            to_column(bias_table.reshape(1, -1), shard_rows),
            w_router,
        ],
        axis=1,
    )
    small = jnp.pad(small, ((0, 0), (0, 128 - small.shape[1])))
    first_all = lax.all_gather(
        jnp.concatenate([w_query, w_key, w_value, small], axis=1), "dp", axis=0, tiled=True
    )
    output_weight = lax.all_gather(w_output, "dp", axis=0, tiled=True)
    attn_width = w_query.shape[1]
    qkv_weight = first_all[:, : 3 * attn_width]
    small_all = first_all[:, 3 * attn_width :]
    gain_attn_all = small_all[:, 0]
    gain_ffn_all = small_all[:, 1]
    table_all = from_column(small_all[:, 2], dp_count, bias_table.shape)
    router_weight = small_all[:, 3 : 3 + expert_count]
    token_count, model_width = inputs.shape
    head_size = attn_width // head_count

    bucket_pick = (
        jnp.arange(bucket_count, dtype=jnp.int32)[:, None] == diagonal_buckets(buckets)[None, :]
    ).astype(jnp.float32)
    diagonals = jnp.einsum(
        "bh,bm->hm", table_all.astype(jnp.float32), bucket_pick, precision=lax.Precision.HIGHEST
    )
    input_float = inputs.astype(jnp.float32)
    attn_gain = gain_attn_all.astype(jnp.float32)
    inverse_attn = lax.rsqrt(jnp.mean(input_float * input_float, axis=-1, keepdims=True) + epsilon)
    normed = (input_float * inverse_attn * attn_gain).astype(jnp.bfloat16)
    qkv = jnp.dot(normed, qkv_weight, preferred_element_type=jnp.float32).astype(jnp.bfloat16)
    attended, log_sums = attend(qkv, diagonals, segments, head_size)
    branch = jnp.dot(attended, output_weight, preferred_element_type=jnp.float32)
    middle = input_float + branch
    ffn_gain = gain_ffn_all.astype(jnp.float32)
    inverse_ffn = lax.rsqrt(jnp.mean(middle * middle, axis=-1, keepdims=True) + epsilon)
    normed2 = (middle * inverse_ffn * ffn_gain).astype(jnp.bfloat16)
    logits = jnp.dot(normed2, router_weight, preferred_element_type=jnp.float32)
    router_probs = jax.nn.softmax(logits, axis=-1)
    route_pick = (routes[:, None] == jnp.arange(expert_count, dtype=jnp.int32)[None, :]).astype(
        jnp.float32
    )
    gate_value = jnp.sum(router_probs * route_pick, axis=-1)
    local_experts = expert_count // group_count
    turn = lax.rem(routes // local_experts - group + group_count, group_count)
    slot_place = (turn * local_experts + lax.rem(routes, local_experts)) * CAP + slot_ids
    dispatch = (
        slot_place[:, None] == jnp.arange(expert_count * CAP, dtype=jnp.int32)[None, :]
    ).astype(jnp.bfloat16)
    block_shape = (group_count, local_experts, CAP, model_width)

    def to_slots(rows):
        return (
            jnp.einsum("ts,td->sd", dispatch, rows, preferred_element_type=jnp.float32)
            .astype(jnp.bfloat16)
            .reshape(block_shape)
        )

    def from_slots(blocks):
        return jnp.dot(
            dispatch,
            blocks.reshape(expert_count * CAP, model_width),
            preferred_element_type=jnp.float32,
        )

    grad_out = cotangent.astype(jnp.float32)
    grad_back = (gate_value[:, None] * grad_out).astype(jnp.bfloat16)
    arrived = exchange(to_slots(normed2), group_count, 1)
    grad_produced = exchange(to_slots(grad_back), group_count, 1)
    arrived_all = lax.all_gather(arrived, "dp", axis=0)
    grad_produced_all = lax.all_gather(grad_produced, "dp", axis=0)
    produced, grad_arrived = expert_rows(arrived, grad_produced, w_in, w_out)
    returned = from_slots(exchange(produced, group_count, -1))
    grad_normed2 = from_slots(exchange(grad_arrived, group_count, -1))
    output = (middle + gate_value[:, None] * returned).astype(jnp.bfloat16)
    grad_gate = jnp.sum(grad_out * returned, axis=-1)
    hidden_part = w_in.shape[1] // dp_count
    grad_w_in, grad_w_out = expert_weight_grads(
        arrived_all,
        grad_produced_all,
        lax.dynamic_slice_in_dim(w_in, shard * hidden_part, hidden_part, 1),
        lax.dynamic_slice_in_dim(w_out, shard * hidden_part, hidden_part, 1),
    )
    grad_probs = route_pick * grad_gate[:, None]
    grad_logits = (
        router_probs * (grad_probs - jnp.sum(router_probs * grad_probs, axis=-1, keepdims=True))
    ).astype(jnp.bfloat16)
    router_local = jnp.einsum("td,te->de", normed2, grad_logits, preferred_element_type=jnp.float32)
    grad_normed2 = grad_normed2 + jnp.einsum(
        "te,de->td", grad_logits, router_weight, preferred_element_type=jnp.float32
    )
    grad_mid_norm, ffn_gain_local = norm_back(grad_normed2, middle, inverse_ffn, ffn_gain)
    grad_middle = grad_out + grad_mid_norm
    grad_branch = grad_middle.astype(jnp.bfloat16)
    output_local = jnp.einsum(
        "tc,td->cd", attended, grad_branch, preferred_element_type=jnp.float32
    )
    grad_attended = jnp.einsum(
        "td,cd->tc", grad_branch, output_weight, preferred_element_type=jnp.float32
    ).astype(jnp.bfloat16)
    grad_q_rows, grad_k_rows, grad_v_rows, grad_diagonals = attend_back(
        qkv, grad_attended, diagonals, segments, log_sums, head_size
    )
    table_local = jnp.einsum(
        "bm,hm->bh", bucket_pick, grad_diagonals, precision=lax.Precision.HIGHEST
    )
    grad_qkv = jnp.concatenate([grad_q_rows, grad_k_rows, grad_v_rows], axis=1)
    qkv_local = jnp.einsum("td,tc->dc", normed, grad_qkv, preferred_element_type=jnp.float32)
    grad_normed = jnp.einsum("tc,dc->td", grad_qkv, qkv_weight, preferred_element_type=jnp.float32)
    grad_in_norm, attn_gain_local = norm_back(grad_normed, input_float, inverse_attn, attn_gain)
    grad_inputs = (grad_middle + grad_in_norm).astype(jnp.bfloat16)
    packed = jnp.concatenate(
        [
            qkv_local,
            output_local,
            attn_gain_local[:, None],
            ffn_gain_local[:, None],
            to_column(table_local.reshape(dp_count, -1), shard_rows),
            router_local,
        ],
        axis=1,
    ).astype(jnp.bfloat16)
    packed = jnp.pad(packed, ((0, 0), (0, -packed.shape[1] % 128)))
    packed = lax.psum_scatter(packed, "dp", scatter_dimension=0, tiled=True)
    packed = lax.psum(packed, "expert").astype(jnp.float32)
    grad_w_query = packed[:, :attn_width]
    grad_w_key = packed[:, attn_width : 2 * attn_width]
    grad_w_value = packed[:, 2 * attn_width : 3 * attn_width]
    grad_w_output = packed[:, 3 * attn_width : 3 * attn_width + model_width]
    rest = packed[:, 3 * attn_width + model_width :]
    grad_gain_attn = rest[:, 0]
    grad_gain_ffn = rest[:, 1]
    grad_bias_table = rest[: bias_table.size, 2].reshape(bias_table.shape)
    grad_w_router = rest[:, 3 : 3 + expert_count]
    return (
        output,
        grad_inputs,
        grad_gain_attn,
        grad_w_query,
        grad_w_key,
        grad_w_value,
        grad_w_output,
        grad_bias_table,
        grad_gain_ffn,
        grad_w_router,
        grad_w_in,
        grad_w_out,
    )


def solution(mesh):
    placed = (
        P(("expert", "dp"), None),
        P("dp"),
        P("dp", None),
        P("dp", None),
        P("dp", None),
        P("dp", None),
        P("dp", None),
        P("dp"),
        P("dp", None),
        P("expert", None, None),
        P("expert", None, None),
        P(("expert", "dp"), None),
        P(),
        P(("expert", "dp")),
        P(("expert", "dp")),
        P(("expert", "dp"), None),
    )
    return jax.shard_map(
        on_device,
        mesh=mesh,
        in_specs=placed,
        out_specs=(
            P(("expert", "dp"), None),
            P(("expert", "dp"), None),
            P("dp"),
            P("dp", None),
            P("dp", None),
            P("dp", None),
            P("dp", None),
            P("dp", None),
            P("dp"),
            P("dp", None),
            P("expert", "dp", None),
            P("expert", "dp", None),
        ),
        check_vma=False,
    )
```
